256 devices in a mesh: dp: 16 (over y, x), seq: 16 (over z, core).
Axes of the slice: x: 4, y: 4, z: 8, core: 2. Of those that a mesh axis runs over, the one named last changes fastest.
Arguments:
- query_rows: bfloat16 [16, 2048, 4096], P('dp', 'seq'), may hold values from -4.5 to 4.5
- key_rows: bfloat16 [16, 2048, 512], P('dp', 'seq'), may hold values from -4.5 to 4.5
- value_rows: bfloat16 [16, 2048, 512], P('dp', 'seq'), may hold values from -6 to 6
- out_grad: bfloat16 [16, 2048, 4096], P('dp', 'seq'), may hold values from -6 to 6
- doc_lengths: int32 [16, 16], replicated, may hold values from 0 to 2048, as said below
Outputs:
- attention: bfloat16 [16, 2048, 4096], P('dp', 'seq')
- query_grad: bfloat16 [16, 2048, 4096], P('dp', 'seq')
- key_grad: bfloat16 [16, 2048, 512], P('dp', 'seq')
- value_grad: bfloat16 [16, 2048, 512], P('dp', 'seq')
The draws below stay inside these ranges and needn't reach their ends.
Inputs may be any that keep to these rules, and one draw needn't show every extreme that they name: `doc_lengths`: row p lists the lengths of the documents packed into pack p: positive lengths first, then zeros, summing to 2048; pack 0 holds a single document.
All inputs are finite; a program needn't handle non-finite values.
Results may differ from the reference program's by a relative error of at most 0.0057.
Values may be sent and summed in bfloat16 or wider, within the bound.
A program may use at most 128 MiB of HBM per device.

```python
from functools import partial
import jax
import jax.numpy as jnp
from jax import lax

QH = 32
KVH = 4
HD = 128
NDOC = 16
PACK = 2048
N_DP = 16


def draw_query_rows(key, part):
    key = jax.random.fold_in(key, 11)
    shape = (N_DP, PACK, QH * HD)
    values = jnp.clip(jax.random.normal(key, shape, jnp.float32), -4.5, 4.5)
    return values.astype(jnp.bfloat16)


def draw_key_rows(key, part):
    key = jax.random.fold_in(key, 12)
    shape = (N_DP, PACK, KVH * HD)
    values = jnp.clip(jax.random.normal(key, shape, jnp.float32), -4.5, 4.5)
    return values.astype(jnp.bfloat16)


def draw_doc_lengths(key, part):
    key = jax.random.fold_in(key, 13)
    count_key, cut_key = jax.random.split(key)
    live_counts = jax.random.randint(count_key, (N_DP,), 2, NDOC + 1).astype(jnp.int32)
    live_counts = live_counts.at[0].set(1)
    row_keys = jax.random.split(cut_key, N_DP)

    def one_row(row_key, live):
        picks = jax.random.permutation(row_key, PACK - 1)[:NDOC - 1].astype(jnp.int32) + 1
        picks = jnp.where(lax.iota(jnp.int32, NDOC - 1) < live - 1, picks, PACK)
        picks = jnp.sort(picks)
        bounds = jnp.concatenate([jnp.zeros((1,), jnp.int32), picks, jnp.full((1,), PACK, jnp.int32)])
        return bounds[1:] - bounds[:-1]
    return jax.vmap(one_row)(row_keys, live_counts).astype(jnp.int32)


def level_of(key, dims, cuts, smallest, top_value):
    level = 1.0
    for axis_at, parts in cuts:
        steps = jax.random.uniform(jax.random.fold_in(jax.random.fold_in(key, 6), axis_at), (parts,), jnp.float32, smallest / len(cuts), top_value / len(cuts))
        level = level * jnp.repeat(jnp.exp(steps), dims[axis_at] // parts).reshape((-1,) + (1,) * (len(dims) - 1 - axis_at))
    return level


def centred(key, dims, deviation, reach, shards=(), held_as=jnp.bfloat16):
    gain = level_of(key, dims, shards, -0.22, 0.18) if shards else 1.0
    entries = jax.random.normal(key, dims, jnp.float32) * deviation * gain
    return jnp.minimum(jnp.maximum(entries, -reach), reach).astype(held_as)


def setup_inputs(seed: int = 0) -> dict:
    keys = jax.random.split(jax.random.key(seed), 6)
    return {
        "query_rows": draw_query_rows(jax.random.fold_in(keys[5], 71), 0),
        "key_rows": draw_key_rows(jax.random.fold_in(keys[5], 71), 0),
        "value_rows": centred(keys[2], (N_DP, PACK, KVH * HD), 1.0, 6.0, ((0, 16), (1, 16))),
        "out_grad": centred(keys[3], (N_DP, PACK, QH * HD), 1.0, 6.0, ((0, 16), (1, 16))),
        "doc_lengths": draw_doc_lengths(jax.random.fold_in(keys[5], 71), 0),
    }


masked_floor = -1.0e30


def pack_segments(length_row):
    finish = jnp.cumsum(length_row).astype(jnp.int32)
    places = jnp.arange(PACK, dtype=jnp.int32)
    return jnp.sum((places[:, None] >= finish[None, :]).astype(jnp.int32), axis=1)


def group_pass(group_inputs, visible):
    query_group, grad_group, key_group, value_group = group_inputs
    factor = HD ** -0.5
    query_wide = query_group.astype(jnp.float32)
    grad_wide = grad_group.astype(jnp.float32)
    key_wide = key_group.astype(jnp.float32)
    value_wide = value_group.astype(jnp.float32)
    scores = jnp.einsum("nqh,kh->nqk", query_wide, key_wide) * factor
    masked = jnp.where(visible[None], scores, masked_floor)
    peaks = jnp.max(masked, axis=-1, keepdims=True)
    raised = jnp.where(visible[None], jnp.exp(masked - peaks), 0.0)
    weight_rows = raised / jnp.sum(raised, axis=-1, keepdims=True)
    weight_half = weight_rows.astype(jnp.bfloat16)
    weight_back = lax.optimization_barrier(weight_half).astype(jnp.float32)
    attended = jnp.einsum("nqk,kh->nqh", weight_back, value_wide)
    row_delta = jnp.sum(grad_wide * attended, axis=-1, keepdims=True)
    dweight = jnp.einsum("nqh,kh->nqk", grad_wide, value_wide)
    dscore_half = (weight_rows * (dweight - row_delta)).astype(jnp.bfloat16)
    dscore = lax.optimization_barrier(dscore_half).astype(jnp.float32)
    query_grad = jnp.einsum("nqk,kh->nqh", dscore, key_wide) * factor
    key_grad = jnp.einsum("nqk,nqh->kh", dscore, query_wide) * factor
    value_grad = jnp.einsum("nqk,nqh->kh", weight_back, grad_wide)
    return (attended.astype(jnp.bfloat16), query_grad.astype(jnp.bfloat16),
            key_grad.astype(jnp.bfloat16), value_grad.astype(jnp.bfloat16))


def one_pack(pack_inputs):
    query_pack, key_pack, value_pack, grad_pack, length_row = pack_inputs
    segment = pack_segments(length_row)
    places = jnp.arange(PACK, dtype=jnp.int32)
    visible = (segment[:, None] == segment[None, :]) & (places[None, :] <= places[:, None])
    per_group = QH // KVH
    query_split = query_pack.reshape(PACK, KVH, per_group, HD).transpose(1, 2, 0, 3)
    grad_split = grad_pack.reshape(PACK, KVH, per_group, HD).transpose(1, 2, 0, 3)
    key_split = key_pack.reshape(PACK, KVH, HD).transpose(1, 0, 2)
    value_split = value_pack.reshape(PACK, KVH, HD).transpose(1, 0, 2)
    attended, query_grad, key_grad, value_grad = lax.map(
        partial(group_pass, visible=visible), (query_split, grad_split, key_split, value_split))
    attention = attended.transpose(2, 0, 1, 3).reshape(PACK, QH * HD)
    query_out = query_grad.transpose(2, 0, 1, 3).reshape(PACK, QH * HD)
    key_out = key_grad.transpose(1, 0, 2).reshape(PACK, KVH * HD)
    value_out = value_grad.transpose(1, 0, 2).reshape(PACK, KVH * HD)
    return attention, query_out, key_out, value_out


def reference(query_rows, key_rows, value_rows, out_grad, doc_lengths):
    attention, query_grad, key_grad, value_grad = lax.map(
        one_pack, (query_rows, key_rows, value_rows, out_grad, doc_lengths))
    return attention, query_grad, key_grad, value_grad
```

```python
import math

import jax
import jax.numpy as jnp
from jax import lax
from jax.experimental import pallas as pl
from jax.experimental.pallas import tpu as pltpu
from jax.sharding import PartitionSpec as P

HD = 128
CHIPS = 8
CORES = 2
GROUPS = 2
GHEADS = 8
ROWS = 128
CHIP_ROWS = CORES * ROWS
HALF = GROUPS * GHEADS * HD
GWIDTH = GHEADS * HD
WIDE = GHEADS * CHIP_ROWS
DOCS = 16
FACTOR = HD**-0.5
EXP_SCALE = FACTOR * math.log2(math.e)
HIDDEN = -1e30
UP, DOWN = 0, 1
HOPS = ((4, 3), (3, 4))
FORWARD_NAMES = ("key", "value")

NT = (((1,), (1,)), ((), ()))
NN = (((1,), (0,)), ((), ()))


def mm(a, b, dims):
    return lax.dot_general(a, b, dims, preferred_element_type=jnp.float32)


def fold_rows(x, op):
    return op(op(x.reshape(x.shape[0] // 8, 8, x.shape[1]), axis=0), axis=0, keepdims=True)


def kernel(
    q_hbm, k_hbm, v_hbm, do_hbm, doc_ref,
    o_hbm, dq_hbm, dk_hbm, dv_hbm,
    q_s, do_s, kv, bias, p_s, scale_s, sum_s, ot_s, dqt_s, delta_s, o_st, dq_st,
    part, outbox, inbox, g_st,
    in_local, in_send, in_recv, ag_send, ag_recv, rs_send, rs_recv,
    out_local, out_send, out_recv,
):
    pack = lax.axis_index("dp")
    place = lax.axis_index("seq")
    z = place // CORES
    core = lax.rem(place, CORES)
    other = 1 - core

    def chip(offset):
        return lax.rem(z + offset + CHIPS, CHIPS)

    sibling = {"seq": z * CORES + other}
    neighbour = ({"seq": chip(1) * CORES + core}, {"seq": chip(-1) * CORES + core})

    barrier = pltpu.get_barrier_semaphore()
    for target in (sibling, *neighbour):
        pl.semaphore_signal(barrier, inc=1, device_id=target, device_id_type=pl.DeviceIdType.MESH)

    def remote(src, dst, send, recv, target):
        return pltpu.make_async_remote_copy(
            src_ref=src, dst_ref=dst, send_sem=send, recv_sem=recv,
            device_id=target, device_id_type=pl.DeviceIdType.MESH,
        )

    def columns(start, width):
        return pl.ds(pl.multiple_of(start, HD), width)

    loads, swaps = {}, {}
    for g in range(GROUPS):
        for n, (src, wide) in enumerate(
            ((k_hbm, HD), (v_hbm, HD), (q_hbm, GWIDTH), (do_hbm, GWIDTH))
        ):
            if n < 2:
                dst = kv.at[n, g, z, core]
            else:
                dst = (q_s, do_s)[n - 2].at[g, core]
            mine = src.at[:, columns((core * GROUPS + g) * wide, wide)]
            theirs = src.at[:, columns((other * GROUPS + g) * wide, wide)]
            loads[n, g] = pltpu.make_async_copy(mine, dst, in_local.at[n, g])
            swaps[n, g] = remote(theirs, dst, in_send.at[n, g], in_recv.at[n, g], sibling)
    for g in range(GROUPS):
        for n in range(4):
            loads[n, g].start()

    pl.semaphore_wait(barrier, 3)
    for key in ((0, 0), (1, 0), (2, 0), (3, 0), (0, 1), (1, 1), (2, 1), (3, 1)):
        swaps[key].start()

    def arrive(n, g):
        loads[n, g].wait()
        if n < 2:
            landed = kv.at[n, g, z, other]
        else:
            landed = (q_s, do_s)[n - 2].at[g, other]
        remote(landed, landed, in_send.at[n, g], in_recv.at[n, g], sibling).wait_recv()

    sent = []

    def gather_send(a, g, way, step):
        block = kv.at[a, g, chip(-step if way == UP else step)]
        copy = remote(
            block, block, ag_send.at[a, g, way, step], ag_recv.at[a, g, way, step], neighbour[way]
        )
        copy.start()
        sent.append(copy)

    def gather_recv(a, g, way, step):
        block = kv.at[a, g, chip(-1 - step if way == UP else 1 + step)]
        remote(
            block, block, ag_send.at[a, g, way, step], ag_recv.at[a, g, way, step], neighbour[way]
        ).wait_recv()

    def gather_step(a, g, step):
        for way in (UP, DOWN):
            if 0 < step <= HOPS[a][way]:
                gather_recv(a, g, way, step - 1)
            if step < HOPS[a][way]:
                gather_send(a, g, way, step)

    def scatter_hops(a, way):
        return HOPS[a][1 - way]

    def scatter_at(a, way, step):
        hops = scatter_hops(a, way)
        return chip(hops - step if way == UP else step - hops)

    def scatter_wait(a, g, way, step):
        box = inbox.at[a, g, way, step]
        remote(
            box, box, rs_send.at[a, g, way, step], rs_recv.at[a, g, way, step], neighbour[way]
        ).wait_recv()

    def scatter_send(a, g, way, step):
        term = part[a, scatter_at(a, way, step)]
        if step > 0:
            scatter_wait(a, g, way, step - 1)
            term = term + inbox[a, g, way, step - 1].astype(jnp.float32)
        outbox[a, g, way, step] = term.astype(jnp.bfloat16)
        copy = remote(
            outbox.at[a, g, way, step], inbox.at[a, g, way, step],
            rs_send.at[a, g, way, step], rs_recv.at[a, g, way, step], neighbour[way],
        )
        copy.start()
        sent.append(copy)

    def scatter_step(a, g, stage):
        for way in (UP, DOWN):
            step = stage - (4 - scatter_hops(a, way))
            if 0 <= step < scatter_hops(a, way):
                scatter_send(a, g, way, step)

    finals = []

    def leave(kind, g, staged, out, wide):
        here = out.at[:, columns((core * GROUPS + g) * wide, wide)]
        local = pltpu.make_async_copy(staged.at[core], here, out_local.at[kind, g])
        far = remote(
            staged.at[other], here, out_send.at[kind, g], out_recv.at[kind, g], sibling
        )
        local.start()
        far.start()
        there = out.at[:, columns((other * GROUPS + g) * wide, wide)]
        finals.append((local, far, kind, g, there))

    def scatter_last(a, g):
        term = part[a, z]
        for way in (UP, DOWN):
            hops = scatter_hops(a, way)
            scatter_wait(a, g, way, hops - 1)
            term = term + inbox[a, g, way, hops - 1].astype(jnp.float32)
        if a == 0:
            term = term * FACTOR
        g_st[a, g] = term.astype(jnp.bfloat16).reshape(CORES, ROWS, HD)
        leave(2 + a, g, g_st.at[a, g], (dk_hbm, dv_hbm)[a], HD)

    def make_bias():
        query = lax.broadcasted_iota(jnp.int32, (1, CHIP_ROWS), 1) + z * CHIP_ROWS
        opening = jnp.zeros((1, CHIP_ROWS), jnp.int32)
        end = jnp.int32(0)
        for d in range(DOCS):
            end = end + doc_ref[pack, d]
            ends = jnp.full((1, CHIP_ROWS), 0, jnp.int32) + end
            opening = jnp.maximum(opening, jnp.where(ends <= query, ends, 0))
        rows = lax.broadcasted_iota(jnp.int32, (CHIP_ROWS, CHIP_ROWS), 0)

        def one(b, carry):
            at = rows + b * CHIP_ROWS
            bias[b] = jnp.where((at >= opening) & (at <= query), 0.0, HIDDEN)
            return carry

        lax.fori_loop(0, CHIPS, one, 0)

    def heads(ref, g):
        parts = [
            ref[g, :, :, h * HD : (h + 1) * HD].reshape(CHIP_ROWS, HD) for h in range(GHEADS)
        ]
        return jnp.concatenate(parts, axis=0)

    def rows_of(a, g, b):
        return kv[a, g, b].reshape(CHIP_ROWS, HD)

    def score_pass(g, blocks):
        for b in blocks:
            hide = jnp.concatenate([bias[b]] * GHEADS, axis=1)
            scores = mm(rows_of(0, g, b), heads(q_s, g), NT) + hide
            peak = fold_rows(scores, jnp.max) * EXP_SCALE
            raised = jnp.exp2(scores * EXP_SCALE - peak)
            p_s[b] = raised
            scale_s[b] = peak
            sum_s[b] = fold_rows(raised, jnp.sum)

    def merge_scales():
        peaks = [scale_s[b] for b in range(CHIPS)]
        top = peaks[0]
        for peak in peaks[1:]:
            top = jnp.maximum(top, peak)
        lifts = [jnp.exp2(peak - top) for peak in peaks]
        total = sum_s[0] * lifts[0]
        for b in range(1, CHIPS):
            total = total + sum_s[b] * lifts[b]
        inverse = 1.0 / total
        for b in range(CHIPS):
            scale_s[b] = lifts[b] * inverse

    def value_pass(g, blocks, first):
        total = None if first else ot_s[...]
        for b in blocks:
            weight = p_s[b] * scale_s[b]
            p_s[b] = weight
            half = weight.astype(jnp.bfloat16)
            term = mm(rows_of(1, g, b).T, half, NN)
            total = term if total is None else total + term
            part[1, b] = mm(half, heads(do_s, g), NN)
        ot_s[...] = total

    def value_end(g):
        for h in range(GHEADS):
            span = slice(h * CHIP_ROWS, (h + 1) * CHIP_ROWS)
            cols = slice(h * HD, (h + 1) * HD)
            out = ot_s[:, span]
            grad = do_s[g, :, :, cols].reshape(CHIP_ROWS, HD).astype(jnp.float32)
            delta_s[:, span] = jnp.sum(out * grad.T, axis=0, keepdims=True)
            o_st[g, :, :, cols] = out.T.astype(jnp.bfloat16).reshape(CORES, ROWS, HD)
        leave(0, g, o_st.at[g], o_hbm, GWIDTH)

    def score_back(g, blocks, first):
        total = None if first else dqt_s[...]
        for b in blocks:
            dweight = mm(rows_of(1, g, b), heads(do_s, g), NT)
            dscore = (p_s[b] * (dweight - delta_s[...])).astype(jnp.bfloat16)
            term = mm(rows_of(0, g, b).T, dscore, NN)
            total = term if total is None else total + term
            part[0, b] = mm(dscore, heads(q_s, g), NN)
        dqt_s[...] = total

    def query_end(g):
        for h in range(GHEADS):
            span = slice(h * CHIP_ROWS, (h + 1) * CHIP_ROWS)
            cols = slice(h * HD, (h + 1) * HD)
            grad = (dqt_s[:, span] * FACTOR).T.astype(jnp.bfloat16)
            dq_st[g, :, :, cols] = grad.reshape(CORES, ROWS, HD)
        leave(1, g, dq_st.at[g], dq_hbm, GWIDTH)

    def at(*offsets):
        return [chip(o) for o in offsets]

    for a in (0, 1):
        arrive(a, 0)
        gather_step(a, 0, 0)
    make_bias()
    arrive(2, 0)
    arrive(3, 0)
    score_pass(0, at(0))
    for a in (0, 1):
        gather_step(a, 0, 1)
    score_pass(0, at(-1, 1))
    for a in (0, 1):
        gather_step(a, 0, 2)
    arrive(0, 1)
    arrive(1, 1)
    score_pass(0, at(-2, 2))
    for a in (0, 1):
        gather_step(a, 0, 3)
    for a in (0, 1):
        gather_step(a, 1, 0)
    score_pass(0, at(-3, 3))
    for a in (0, 1):
        gather_step(a, 0, 4)
    score_pass(0, at(4))
    merge_scales()

    value_pass(0, at(4, 3), True)
    scatter_step(1, 0, 0)
    for a in (0, 1):
        gather_step(a, 1, 1)
    value_pass(0, at(-3, 2), False)
    value_pass(0, at(-2, 1), False)
    for a in (0, 1):
        gather_step(a, 1, 2)
    scatter_step(1, 0, 1)
    value_pass(0, at(-1, 0), False)
    value_end(0)

    score_back(0, at(4, -3), True)
    scatter_step(1, 0, 2)
    scatter_step(0, 0, 0)
    for a in (0, 1):
        gather_step(a, 1, 3)
    score_back(0, at(3, -2), False)
    scatter_step(1, 0, 3)
    score_back(0, at(2, -1), False)
    scatter_step(0, 0, 1)
    score_back(0, at(1, 0), False)
    for a in (0, 1):
        gather_step(a, 1, 4)
    scatter_last(1, 0)
    query_end(0)

    arrive(2, 1)
    arrive(3, 1)
    score_pass(1, at(0, -1, 1, -2))
    scatter_step(0, 0, 2)
    score_pass(1, at(2, -3, 3, 4))
    scatter_step(0, 0, 3)
    merge_scales()
    value_pass(1, at(4, 3), True)
    scatter_step(1, 1, 0)
    value_pass(1, at(-3, 2), False)
    scatter_last(0, 0)
    scatter_step(1, 1, 1)
    value_pass(1, at(-2, 1), False)
    value_pass(1, at(-1, 0), False)
    scatter_step(1, 1, 2)
    value_end(1)
    score_back(1, at(4, -3), True)
    scatter_step(0, 1, 0)
    score_back(1, at(3, -2), False)
    scatter_step(1, 1, 3)
    scatter_step(0, 1, 1)
    score_back(1, at(2, -1), False)
    scatter_step(0, 1, 2)
    score_back(1, at(1, 0), False)
    scatter_step(0, 1, 3)
    query_end(1)
    scatter_last(1, 1)
    scatter_last(0, 1)

    for copy in swaps.values():
        copy.wait_send()
    for copy in sent:
        copy.wait_send()
    for local_copy, far, kind, g, there in finals:
        local_copy.wait()
        far.wait_send()
        remote(
            there, there, out_send.at[kind, g], out_recv.at[kind, g], sibling
        ).wait_recv()


def local(query_rows, key_rows, value_rows, out_grad, doc_lengths):
    rows = query_rows.shape[1]
    half = jnp.bfloat16
    flat = [x.reshape(rows, x.shape[2]) for x in (query_rows, key_rows, value_rows, out_grad)]
    anywhere = pl.BlockSpec(memory_space=pl.ANY)
    dma = pltpu.SemaphoreType.DMA
    outs = pl.pallas_call(
        kernel,
        out_shape=[
            jax.ShapeDtypeStruct(flat[0].shape, half),
            jax.ShapeDtypeStruct(flat[0].shape, half),
            jax.ShapeDtypeStruct(flat[1].shape, half),
            jax.ShapeDtypeStruct(flat[1].shape, half),
        ],
        in_specs=[anywhere] * 4 + [pl.BlockSpec(memory_space=pltpu.SMEM)],
        out_specs=[anywhere] * 4,
        scratch_shapes=[
            pltpu.VMEM((GROUPS, CORES, ROWS, GWIDTH), half),
            pltpu.VMEM((GROUPS, CORES, ROWS, GWIDTH), half),
            pltpu.VMEM((2, GROUPS, CHIPS, CORES, ROWS, HD), half),
            pltpu.VMEM((CHIPS, CHIP_ROWS, CHIP_ROWS), jnp.float32),
            pltpu.VMEM((CHIPS, CHIP_ROWS, WIDE), jnp.float32),
            pltpu.VMEM((CHIPS, 1, WIDE), jnp.float32),
            pltpu.VMEM((CHIPS, 1, WIDE), jnp.float32),
            pltpu.VMEM((HD, WIDE), jnp.float32),
            pltpu.VMEM((HD, WIDE), jnp.float32),
            pltpu.VMEM((1, WIDE), jnp.float32),
            pltpu.VMEM((GROUPS, CORES, ROWS, GWIDTH), half),
            pltpu.VMEM((GROUPS, CORES, ROWS, GWIDTH), half),
            pltpu.VMEM((2, CHIPS, CHIP_ROWS, HD), jnp.float32),
            pltpu.VMEM((2, GROUPS, 2, 4, CHIP_ROWS, HD), half),
            pltpu.VMEM((2, GROUPS, 2, 4, CHIP_ROWS, HD), half),
            pltpu.VMEM((2, GROUPS, CORES, ROWS, HD), half),
            dma((4, GROUPS)), dma((4, GROUPS)), dma((4, GROUPS)),
            dma((2, GROUPS, 2, 4)), dma((2, GROUPS, 2, 4)),
            dma((2, GROUPS, 2, 4)), dma((2, GROUPS, 2, 4)),
            dma((4, GROUPS)), dma((4, GROUPS)), dma((4, GROUPS)),
        ],
        compiler_params=pltpu.CompilerParams(
            collective_id=0, has_side_effects=True, vmem_limit_bytes=60 * 2**20
        ),
        name="packed_attention",
    )(*flat, doc_lengths)
    return tuple(x.reshape(1, rows, x.shape[1]) for x in outs)


def solution(mesh):
    placed = P("dp", "seq", None)
    return jax.shard_map(
        local,
        mesh=mesh,
        in_specs=(placed,) * 4 + (P(),),
        out_specs=(placed,) * 4,
        check_vma=False,
    )
```

```python
import math

import jax
import jax.numpy as jnp
from jax import lax
from jax.experimental import pallas as pl
from jax.experimental.pallas import tpu as pltpu
from jax.sharding import PartitionSpec as P

HD = 128
CHIPS = 8
CORES = 2
GROUPS = 2
GHEADS = 8
ROWS = 128
CHIP_ROWS = CORES * ROWS
HALF = GROUPS * GHEADS * HD
GWIDTH = GHEADS * HD
WIDE = GHEADS * CHIP_ROWS
DOCS = 16
FACTOR = HD**-0.5
EXP_SCALE = FACTOR * math.log2(math.e)
HIDDEN = -1e30
UP, DOWN = 0, 1
HOPS = (4, 3)
COMING = ((0, 1), (6, 7), (2, 3), (4, 5))
GOING = ((4, 5), (2, 3), (6, 7), (0, 1))
EVENTS = {
    ("value", 0, 0): ((1, 0, 0),),
    ("value", 0, 3): ((1, 0, 1),),
    ("score", 0, 0): ((0, 0, 0),),
    ("score", 0, 1): ((1, 0, 2),),
    ("score", 0, 2): ((0, 0, 1),),
    ("score", 0, 3): ((1, 0, 3),),
    ("value", 1, 0): ((1, 1, 0),),
    ("value", 1, 1): ((1, 0, 4),),
    ("value", 1, 2): ((0, 0, 3),),
    ("value", 1, 3): ((1, 1, 1),),
    ("score", 1, 1): ((1, 1, 2), (0, 0, 4)),
    ("score", 1, 3): ((1, 1, 3),),
}
AHEAD = {("value", 0, 0): 1, ("value", 0, 3): 2, ("score", 0, 1): 3}

NT = (((1,), (1,)), ((), ()))
NN = (((1,), (0,)), ((), ()))


def mm(a, b, dims):
    return lax.dot_general(a, b, dims, preferred_element_type=jnp.float32)


def fold_rows(x, op):
    return op(op(x.reshape(x.shape[0] // 8, 8, x.shape[1]), axis=0), axis=0, keepdims=True)


def kernel(
    q_hbm, k_hbm, v_hbm, do_hbm, doc_ref,
    o_hbm, dq_hbm, dk_hbm, dv_hbm,
    q_s, do_s, kv, bias, p_s, scale_s, sum_s, ot_s, dqt_s, delta_s, o_st, dq_st,
    part, own, outbox, inbox, g_st,
    in_local, in_send, in_recv, ag_send, ag_recv, rs_send, rs_recv,
    out_local, out_send, out_recv,
):
    pack = lax.axis_index("dp")
    place = lax.axis_index("seq")
    z = place // CORES
    core = lax.rem(place, CORES)
    other = 1 - core

    def back(d):
        return lax.rem(z - d + CHIPS, CHIPS)

    sibling = {"seq": z * CORES + other}

    def on_chip(c):
        return {"seq": c * CORES + core}

    barrier = pltpu.get_barrier_semaphore()

    def greet(target):
        pl.semaphore_signal(barrier, inc=1, device_id=target, device_id_type=pl.DeviceIdType.MESH)

    greet(sibling)
    for d in range(1, CHIPS):
        greet(on_chip(back(d)))

    def remote(src, dst, send, recv, target):
        return pltpu.make_async_remote_copy(
            src_ref=src, dst_ref=dst, send_sem=send, recv_sem=recv,
            device_id=target, device_id_type=pl.DeviceIdType.MESH,
        )

    def columns(start, width):
        return pl.ds(pl.multiple_of(start, HD), width)

    loads, swaps = {}, {}
    for g in range(GROUPS):
        for n, (src, wide) in enumerate(
            ((k_hbm, HD), (v_hbm, HD), (q_hbm, GWIDTH), (do_hbm, GWIDTH))
        ):
            if n < 2:
                dst = kv.at[g, z, n, core]
            else:
                dst = (q_s, do_s)[n - 2].at[g, core]
            mine = src.at[:, columns((core * GROUPS + g) * wide, wide)]
            theirs = src.at[:, columns((other * GROUPS + g) * wide, wide)]
            loads[n, g] = pltpu.make_async_copy(mine, dst, in_local.at[n, g])
            swaps[n, g] = remote(theirs, dst, in_send.at[n, g], in_recv.at[n, g], sibling)
    order = ((0, 0), (1, 0), (2, 0), (3, 0), (0, 1), (1, 1), (2, 1), (3, 1))
    for key in order:
        loads[key].start()

    pl.semaphore_wait(barrier, CHIPS)
    for key in order:
        swaps[key].start()

    def arrive(n, g):
        loads[n, g].wait()
        if n < 2:
            landed = kv.at[g, z, n, other]
        else:
            landed = (q_s, do_s)[n - 2].at[g, other]
        remote(landed, landed, in_send.at[n, g], in_recv.at[n, g], sibling).wait_recv()

    def ring_hop(g, way, step, source, target):
        block = kv.at[g, source]
        return remote(
            block, block, ag_send.at[g, way, step], ag_recv.at[g, way, step], on_chip(target)
        )

    def ring_sends(way, step):
        if way == UP:
            return (z >= step) & (z < CHIPS - 1)
        return back(-step) <= HOPS[DOWN] - 1

    def ring_out(g, way, step):
        source = back(step if way == UP else -step)
        return ring_hop(g, way, step, source, back(-1 if way == UP else 1))

    def ring(g, step):
        for way in (UP, DOWN):
            if 0 < step <= HOPS[way]:
                coming = z >= step if way == UP else back(-step) <= HOPS[DOWN] - 1

                @pl.when(coming)
                def _():
                    source = back(step if way == UP else -step)
                    ring_hop(g, way, step - 1, source, back(1 if way == UP else -1)).wait_recv()

            if step < HOPS[way]:

                @pl.when(ring_sends(way, step))
                def _():
                    ring_out(g, way, step).start()

    def ring_end(g):
        for way in (UP, DOWN):
            for step in range(HOPS[way]):

                @pl.when(ring_sends(way, step))
                def _():
                    ring_out(g, way, step).wait_send()

    def slot(way, step):
        return way * 4 + step

    def chain_hops(way):
        return HOPS[1 - way]

    def chain_block(way, step):
        left = chain_hops(way) - step
        return back(left if way == DOWN else -left)

    def chain_on(way, step):
        if way == DOWN:
            return z >= chain_hops(way) - step
        return chain_block(way, step) <= chain_hops(way) - 1

    def chain_copy(a, g, way, step):
        at = slot(way, step)
        return remote(
            outbox.at[a, g, at], inbox.at[a, g, at], rs_send.at[a, g, at], rs_recv.at[a, g, at],
            on_chip(back(1 if way == DOWN else -1)),
        )

    def chain_wait(a, g, way, step):
        at = slot(way, step)
        box = inbox.at[a, g, at]
        remote(
            box, box, rs_send.at[a, g, at], rs_recv.at[a, g, at],
            on_chip(back(-1 if way == DOWN else 1)),
        ).wait_recv()

    def chain_step(a, g, way, step):
        at = slot(way, step)
        block = chain_block(way, step)

        def send(term):
            outbox[a, g, at] = term.astype(jnp.bfloat16)
            chain_copy(a, g, way, step).start()

        def both():
            chain_wait(a, g, way, step - 1)
            send(part[a, block] + inbox[a, g, at - 1].astype(jnp.float32))

        on = chain_on(way, step)
        if step == 0:

            @pl.when(on)
            def _():
                send(part[a, block])

        elif way == DOWN:

            @pl.when(on & (z < CHIPS - 1))
            def _():
                both()

            @pl.when(on & (z == CHIPS - 1))
            def _():
                send(part[a, block])

        else:

            @pl.when(on & (z >= block))
            def _():
                both()

            @pl.when(on & (z < block))
            def _():
                chain_wait(a, g, way, step - 1)
                outbox[a, g, at] = inbox[a, g, at - 1]
                chain_copy(a, g, way, step).start()

    def chain(a, g, stage):
        for way in (DOWN, UP):
            if stage < chain_hops(way):
                chain_step(a, g, way, stage)

    def chain_end(a, g):
        for way in (DOWN, UP):
            for step in range(chain_hops(way)):

                @pl.when(chain_on(way, step))
                def _():
                    chain_copy(a, g, way, step).wait_send()

    def term_copy(a, g, target):
        return remote(
            outbox.at[a, g, target], inbox.at[a, g, z],
            rs_send.at[a, g, target], rs_recv.at[a, g, z], on_chip(target),
        )

    def direct(a, g):
        return (a, g) == (0, GROUPS - 1)

    def term_out(a, g, d, term):
        if d == 0:
            own[a, g] = term
        elif direct(a, g):
            outbox[a, g, back(d)] = term.astype(jnp.bfloat16)
        else:
            part[a, back(d)] = term

    def term_send(a, g, blocks):
        for d in blocks:
            if d > 0 and direct(a, g):

                @pl.when(z >= d)
                def _():
                    term_copy(a, g, z - d).start()

    def term_end(a, g):
        if not direct(a, g):
            chain_end(a, g)
            return

        def one(i, carry):
            term_copy(a, g, i).wait_send()
            return carry

        lax.fori_loop(0, z, one, 0)

    finals = []

    def leave(kind, g, staged, out, wide):
        here = out.at[:, columns((core * GROUPS + g) * wide, wide)]
        local = pltpu.make_async_copy(staged.at[core], here, out_local.at[kind, g])
        far = remote(
            staged.at[other], here, out_send.at[kind, g], out_recv.at[kind, g], sibling
        )
        local.start()
        far.start()
        there = out.at[:, columns((other * GROUPS + g) * wide, wide)]
        finals.append((local, far, kind, g, there))

    def term_sum(a, g):
        def add(at):
            own[a, g] = own[a, g] + inbox[a, g, at].astype(jnp.float32)

        def one(i, carry):
            source = CHIPS - 1 - i
            box = inbox.at[a, g, source]
            remote(
                box, box, rs_send.at[a, g, source], rs_recv.at[a, g, source], on_chip(source)
            ).wait_recv()
            add(source)
            return carry

        if direct(a, g):
            lax.fori_loop(0, CHIPS - 1 - z, one, 0)
        else:
            for way, last in ((DOWN, CHIPS - 1), (UP, chain_hops(UP))):

                @pl.when(z < last)
                def _():
                    step = chain_hops(way) - 1
                    chain_wait(a, g, way, step)
                    add(slot(way, step))

        total = own[a, g]
        if a == 0:
            total = total * FACTOR
        g_st[a, g] = total.astype(jnp.bfloat16).reshape(CORES, ROWS, HD)
        leave(2 + a, g, g_st.at[a, g], (dk_hbm, dv_hbm)[a], HD)

    def term_last(a, g, _):
        term_sum(a, g)

    def make_bias():
        query = lax.broadcasted_iota(jnp.int32, (1, CHIP_ROWS), 1) + z * CHIP_ROWS
        opening = jnp.zeros((1, CHIP_ROWS), jnp.int32)
        end = jnp.int32(0)
        for d in range(DOCS):
            end = end + doc_ref[pack, d]
            ends = jnp.full((1, CHIP_ROWS), 0, jnp.int32) + end
            opening = jnp.maximum(opening, jnp.where(ends <= query, ends, 0))
        rows = lax.broadcasted_iota(jnp.int32, (CHIP_ROWS, CHIP_ROWS), 0)

        def one(b, carry):
            at = rows + b * CHIP_ROWS
            bias[b] = jnp.where((at >= opening) & (at <= query), 0.0, HIDDEN)
            return carry

        lax.fori_loop(0, CHIPS, one, 0)

    def clear(i, carry):
        for g in range(GROUPS):
            kv[g, i] = jnp.zeros(kv.shape[2:], kv.dtype)
        return carry

    def heads(ref, g):
        parts = [
            ref[g, :, :, h * HD : (h + 1) * HD].reshape(CHIP_ROWS, HD) for h in range(GHEADS)
        ]
        return jnp.concatenate(parts, axis=0)

    def rows_of(a, g, b):
        return kv[g, b, a].reshape(CHIP_ROWS, HD)

    def score_pass(g, blocks):
        @pl.when(z >= blocks[0])
        def _():
            for d in blocks:
                b = back(d)
                hide = jnp.concatenate([bias[b]] * GHEADS, axis=1)
                scores = mm(rows_of(0, g, b), heads(q_s, g), NT) + hide
                peak = fold_rows(scores, jnp.max) * EXP_SCALE
                raised = jnp.exp2(scores * EXP_SCALE - peak)
                p_s[b] = raised
                scale_s[b] = peak
                sum_s[b] = fold_rows(raised, jnp.sum)

        if blocks[0] > 0:

            @pl.when(z < blocks[0])
            def _():
                for d in blocks:
                    b = back(d)
                    scale_s[b] = jnp.full(scale_s.shape[1:], HIDDEN, jnp.float32)
                    sum_s[b] = jnp.zeros(sum_s.shape[1:], jnp.float32)

    def merge_scales():
        peaks = [scale_s[b] for b in range(CHIPS)]
        top = peaks[0]
        for peak in peaks[1:]:
            top = jnp.maximum(top, peak)
        lifts = [jnp.exp2(peak - top) for peak in peaks]
        total = sum_s[0] * lifts[0]
        for b in range(1, CHIPS):
            total = total + sum_s[b] * lifts[b]
        inverse = 1.0 / total
        for b in range(CHIPS):
            scale_s[b] = lifts[b] * inverse

    def value_pass(g, blocks):
        @pl.when(z >= blocks[0])
        def _():
            total = ot_s[...]
            for d in blocks:
                b = back(d)
                weight = p_s[b] * scale_s[b]
                half = weight.astype(jnp.bfloat16)
                total = total + mm(rows_of(1, g, b).T, half, NN)
                term_out(1, g, d, mm(half, heads(do_s, g), NN))
            ot_s[...] = total

        term_send(1, g, blocks)

    def value_end(g):
        for h in range(GHEADS):
            span = slice(h * CHIP_ROWS, (h + 1) * CHIP_ROWS)
            cols = slice(h * HD, (h + 1) * HD)
            out = ot_s[:, span]
            grad = do_s[g, :, :, cols].reshape(CHIP_ROWS, HD).astype(jnp.float32)
            delta_s[:, span] = jnp.sum(out * grad.T, axis=0, keepdims=True)
            o_st[g, :, :, cols] = out.T.astype(jnp.bfloat16).reshape(CORES, ROWS, HD)
        leave(0, g, o_st.at[g], o_hbm, GWIDTH)

    def score_back(g, blocks):
        @pl.when(z >= blocks[0])
        def _():
            total = dqt_s[...]
            for d in blocks:
                b = back(d)
                dweight = mm(rows_of(1, g, b), heads(do_s, g), NT)
                weight = p_s[b] * scale_s[b]
                dscore = (weight * (dweight - delta_s[...])).astype(jnp.bfloat16)
                total = total + mm(rows_of(0, g, b).T, dscore, NN)
                term_out(0, g, d, mm(dscore, heads(q_s, g), NN))
            dqt_s[...] = total

        term_send(0, g, blocks)

    def query_end(g):
        for h in range(GHEADS):
            span = slice(h * CHIP_ROWS, (h + 1) * CHIP_ROWS)
            cols = slice(h * HD, (h + 1) * HD)
            grad = (dqt_s[:, span] * FACTOR).T.astype(jnp.bfloat16)
            dq_st[g, :, :, cols] = grad.reshape(CORES, ROWS, HD)
        leave(1, g, dq_st.at[g], dq_hbm, GWIDTH)

    for a in (0, 1):
        arrive(a, 0)
    ring(0, 0)
    make_bias()
    lax.fori_loop(jnp.maximum(z + 1, HOPS[DOWN]), CHIPS, clear, 0)
    for n in (2, 3):
        arrive(n, 0)
    ring(0, 1)
    for a in (0, 1):
        arrive(a, 1)
    for step, blocks in enumerate(COMING):
        score_pass(0, blocks)
        if step < 3:
            ring(0, step + 2)
        if step == 1:
            ring(1, 0)
    merge_scales()
    def after(what, g, n):
        if (what, g, n) in AHEAD:
            ring(1, AHEAD[what, g, n])
        for event in EVENTS.get((what, g, n), ()):
            (chain if event[2] < 4 else term_last)(*event)

    for g in range(GROUPS):
        ot_s[...] = jnp.zeros_like(ot_s)
        dqt_s[...] = jnp.zeros_like(dqt_s)
        for n, blocks in enumerate(GOING):
            value_pass(g, blocks)
            after("value", g, n)
        value_end(g)
        for n, blocks in enumerate(GOING):
            score_back(g, blocks)
            after("score", g, n)
        query_end(g)
        if g == 0:
            arrive(2, 1)
            arrive(3, 1)
            ring(1, 4)
            for blocks in COMING:
                score_pass(1, blocks)
            merge_scales()
            chain(0, 0, 2)
    term_sum(1, 1)
    term_sum(0, 1)

    for copy in swaps.values():
        copy.wait_send()
    for g in range(GROUPS):
        ring_end(g)
        for a in (0, 1):
            term_end(a, g)
    for local_copy, far, kind, g, there in finals:
        local_copy.wait()
        far.wait_send()
        remote(
            there, there, out_send.at[kind, g], out_recv.at[kind, g], sibling
        ).wait_recv()


def copy_out(*refs):
    count = (len(refs) - 2) // 3
    ins, outs, held = refs[:count], refs[count : 2 * count], refs[2 * count : 3 * count]
    in_sem, out_sem = refs[-2:]
    reads = [pltpu.make_async_copy(ins[i], held[i], in_sem.at[i]) for i in range(count)]
    writes = [pltpu.make_async_copy(held[i], outs[i], out_sem.at[i]) for i in range(count)]
    for read in reads:
        read.start()
    for read, write in zip(reads, writes):
        read.wait()
        write.start()
    for write in writes:
        write.wait()


def local(query_rows, key_rows, value_rows, out_grad, doc_lengths):
    rows = query_rows.shape[1]
    half = jnp.bfloat16
    flat = [x.reshape(rows, x.shape[2]) for x in (query_rows, key_rows, value_rows, out_grad)]
    anywhere = pl.BlockSpec(memory_space=pl.ANY)
    dma = pltpu.SemaphoreType.DMA
    outs = pl.pallas_call(
        kernel,
        out_shape=[
            jax.ShapeDtypeStruct(flat[0].shape, half),
            jax.ShapeDtypeStruct(flat[0].shape, half),
            jax.ShapeDtypeStruct(flat[1].shape, half),
            jax.ShapeDtypeStruct(flat[1].shape, half),
        ],
        in_specs=[anywhere] * 4 + [pl.BlockSpec(memory_space=pltpu.SMEM)],
        out_specs=[anywhere] * 4,
        scratch_shapes=[
            pltpu.VMEM((GROUPS, CORES, ROWS, GWIDTH), half),
            pltpu.VMEM((GROUPS, CORES, ROWS, GWIDTH), half),
            pltpu.VMEM((GROUPS, CHIPS, 2, CORES, ROWS, HD), half),
            pltpu.VMEM((CHIPS, CHIP_ROWS, CHIP_ROWS), jnp.float32),
            pltpu.VMEM((CHIPS, CHIP_ROWS, WIDE), jnp.float32),
            pltpu.VMEM((CHIPS, 1, WIDE), jnp.float32),
            pltpu.VMEM((CHIPS, 1, WIDE), jnp.float32),
            pltpu.VMEM((HD, WIDE), jnp.float32),
            pltpu.VMEM((HD, WIDE), jnp.float32),
            pltpu.VMEM((1, WIDE), jnp.float32),
            pltpu.VMEM((GROUPS, CORES, ROWS, GWIDTH), half),
            pltpu.VMEM((GROUPS, CORES, ROWS, GWIDTH), half),
            pltpu.VMEM((2, CHIPS, CHIP_ROWS, HD), jnp.float32),
            pltpu.VMEM((2, GROUPS, CHIP_ROWS, HD), jnp.float32),
            pltpu.VMEM((2, GROUPS, CHIPS, CHIP_ROWS, HD), half),
            pltpu.VMEM((2, GROUPS, CHIPS, CHIP_ROWS, HD), half),
            pltpu.VMEM((2, GROUPS, CORES, ROWS, HD), half),
            dma((4, GROUPS)), dma((4, GROUPS)), dma((4, GROUPS)),
            dma((GROUPS, 2, 4)), dma((GROUPS, 2, 4)),
            dma((2, GROUPS, CHIPS)), dma((2, GROUPS, CHIPS)),
            dma((4, GROUPS)), dma((4, GROUPS)), dma((4, GROUPS)),
        ],
        compiler_params=pltpu.CompilerParams(
            collective_id=0, has_side_effects=True, vmem_limit_bytes=60 * 2**20
        ),
        name="packed_attention",
    )(*flat, doc_lengths)
    outs = pl.pallas_call(
        copy_out,
        out_shape=[jax.ShapeDtypeStruct(x.shape, x.dtype) for x in outs],
        in_specs=[anywhere] * 4,
        out_specs=[anywhere] * 4,
        scratch_shapes=[pltpu.VMEM(x.shape, x.dtype) for x in outs] + [dma((4,)), dma((4,))],
        name="copy_out",
    )(*outs)
    return tuple(x.reshape(1, rows, x.shape[1]) for x in outs)


def solution(mesh):
    placed = P("dp", "seq", None)
    return jax.shard_map(
        local,
        mesh=mesh,
        in_specs=(placed,) * 4 + (P(),),
        out_specs=(placed,) * 4,
        check_vma=False,
    )
```

```python
import math

import jax
import jax.numpy as jnp
from jax import lax
from jax.experimental import pallas as pl
from jax.experimental.pallas import tpu as pltpu
from jax.sharding import PartitionSpec as P

HD = 128
CHIPS = 8
CORES = 2
GROUPS = 2
GHEADS = 8
ROWS = 128
CHIP_ROWS = CORES * ROWS
HALF = GROUPS * GHEADS * HD
GWIDTH = GHEADS * HD
WIDE = GHEADS * CHIP_ROWS
DOCS = 16
FACTOR = HD**-0.5
EXP_SCALE = FACTOR * math.log2(math.e)
HIDDEN = -1e30
UP, DOWN = 0, 1
HOPS = (4, 3)
FAR = (5, 6, 7)
COMING = ((0, 1), (6, 7), (2, 3), (4, 5))
GOING = ((4, 5), (2, 3), (6, 7), (0, 1))
EVENTS = {
    ("value", 0, 0): ((1, 0, 0),),
    ("value", 0, 3): ((1, 0, 1),),
    ("score", 0, 0): ((0, 0, 0),),
    ("score", 0, 1): ((1, 0, 2),),
    ("score", 0, 2): ((0, 0, 1),),
    ("score", 0, 3): ((1, 0, 3),),
    ("value", 1, 0): ((1, 1, 0),),
    ("value", 1, 1): ((1, 0, 4),),
    ("value", 1, 2): ((0, 0, 3),),
    ("value", 1, 3): ((1, 1, 1),),
    ("score", 1, 1): ((1, 1, 2), (0, 0, 4)),
    ("score", 1, 3): ((1, 1, 3),),
}
AHEAD = {("value", 0, 0): 1, ("value", 0, 3): 2, ("score", 0, 1): 3}

NT = (((1,), (1,)), ((), ()))
NN = (((1,), (0,)), ((), ()))


def mm(a, b, dims):
    return lax.dot_general(a, b, dims, preferred_element_type=jnp.float32)


def fold_rows(x, op):
    return op(op(x.reshape(x.shape[0] // 8, 8, x.shape[1]), axis=0), axis=0, keepdims=True)


def kernel(
    q_hbm, k_hbm, v_hbm, do_hbm, doc_ref,
    o_hbm, dq_hbm, dk_hbm, dv_hbm,
    q_s, do_s, kv, bias, p_s, scale_s, sum_s, ot_s, dqt_s, delta_s, o_st, dq_st,
    part, own, outbox, inbox, g_st,
    in_local, in_send, in_recv, ag_send, ag_recv, rs_send, rs_recv,
    out_local, out_send, out_recv,
    last_in, last_sums, last_send, last_recv, last_out, dscore_s, first_send, first_recv,
):
    pack = lax.axis_index("dp")
    place = lax.axis_index("seq")
    z = place // CORES
    core = lax.rem(place, CORES)
    other = 1 - core

    def back(d):
        return lax.rem(z - d + CHIPS, CHIPS)

    sibling = {"seq": z * CORES + other}

    def on_chip(c):
        return {"seq": c * CORES + core}

    barrier = pltpu.get_barrier_semaphore()

    def greet(target):
        pl.semaphore_signal(barrier, inc=1, device_id=target, device_id_type=pl.DeviceIdType.MESH)

    greet(sibling)
    for d in range(1, CHIPS):
        for half in range(CORES):
            greet({"seq": back(d) * CORES + half})

    def remote(src, dst, send, recv, target):
        return pltpu.make_async_remote_copy(
            src_ref=src, dst_ref=dst, send_sem=send, recv_sem=recv,
            device_id=target, device_id_type=pl.DeviceIdType.MESH,
        )

    def columns(start, width):
        return pl.ds(pl.multiple_of(start, HD), width)

    loads, swaps = {}, {}
    for g in range(GROUPS):
        for n, (src, wide) in enumerate(
            ((k_hbm, HD), (v_hbm, HD), (q_hbm, GWIDTH), (do_hbm, GWIDTH))
        ):
            if n < 2:
                dst = kv.at[g, z, n, core]
            else:
                dst = (q_s, do_s)[n - 2].at[g, core]
            mine = src.at[:, columns((core * GROUPS + g) * wide, wide)]
            theirs = src.at[:, columns((other * GROUPS + g) * wide, wide)]
            loads[n, g] = pltpu.make_async_copy(mine, dst, in_local.at[n, g])
            swaps[n, g] = remote(theirs, dst, in_send.at[n, g], in_recv.at[n, g], sibling)
    order = ((0, 0), (1, 0), (2, 0), (3, 0), (0, 1), (1, 1), (2, 1), (3, 1))
    for key in order:
        loads[key].start()


    def arrive(n, g):
        loads[n, g].wait()
        if n < 2:
            landed = kv.at[g, z, n, other]
        else:
            landed = (q_s, do_s)[n - 2].at[g, other]
        remote(landed, landed, in_send.at[n, g], in_recv.at[n, g], sibling).wait_recv()

    def ring_hop(g, way, step, source, target):
        block = kv.at[g, source]
        return remote(
            block, block, ag_send.at[g, way, step], ag_recv.at[g, way, step], on_chip(target)
        )

    def first_hop(way, n, half):
        return remote(
            (k_hbm, v_hbm)[n].at[:, columns(half * GROUPS * HD, HD)],
            kv.at[0, z, n, core],
            first_send.at[way, n, half],
            first_recv.at[way, n, core],
            {"seq": back(-1 if way == UP else 1) * CORES + half},
        )

    def first_wait(way, n, half):
        source = back(1 if way == UP else -1)
        block = kv.at[0, source, n, half]
        remote(
            block, block, first_send.at[way, n, half], first_recv.at[way, n, half],
            {"seq": source * CORES + half},
        ).wait_recv()

    def ring_sends(way, step):
        if way == UP:
            return (z >= step) & (z < CHIPS - 1)
        return back(-step) <= HOPS[DOWN] - 1

    def ring_out(g, way, step):
        source = back(step if way == UP else -step)
        return ring_hop(g, way, step, source, back(-1 if way == UP else 1))

    def ring(g, step):
        for way in (UP, DOWN):
            if 0 < step <= HOPS[way]:
                coming = z >= step if way == UP else back(-step) <= HOPS[DOWN] - 1

                @pl.when(coming)
                def _():
                    if (g, step) == (0, 1):
                        for n in (0, 1):
                            for half in range(CORES):
                                first_wait(way, n, half)
                        return
                    source = back(step if way == UP else -step)
                    ring_hop(g, way, step - 1, source, back(1 if way == UP else -1)).wait_recv()

            if step < HOPS[way]:

                @pl.when(ring_sends(way, step))
                def _():
                    if (g, step) == (0, 0):
                        for n in (0, 1):
                            for half in range(CORES):
                                first_hop(way, n, half).start()
                        return
                    ring_out(g, way, step).start()

    def ring_end(g):
        for way in (UP, DOWN):
            for step in range(HOPS[way]):

                @pl.when(ring_sends(way, step))
                def _():
                    if (g, step) == (0, 0):
                        for n in (0, 1):
                            for half in range(CORES):
                                first_hop(way, n, half).wait_send()
                        return
                    ring_out(g, way, step).wait_send()

    def slot(way, step):
        return step

    def chain_hops(way):
        return HOPS[1 - way]

    def chain_block(way, step):
        left = chain_hops(way) - step
        return back(left if way == DOWN else -left)

    def chain_on(way, step):
        if way == DOWN:
            return z >= chain_hops(way) - step
        return chain_block(way, step) <= chain_hops(way) - 1

    def chain_copy(a, g, way, step):
        at = slot(way, step)
        return remote(
            outbox.at[a, g, at], inbox.at[a, g, at], rs_send.at[a, g, at], rs_recv.at[a, g, at],
            on_chip(back(1 if way == DOWN else -1)),
        )

    def chain_wait(a, g, way, step):
        at = slot(way, step)
        box = inbox.at[a, g, at]
        remote(
            box, box, rs_send.at[a, g, at], rs_recv.at[a, g, at],
            on_chip(back(-1 if way == DOWN else 1)),
        ).wait_recv()

    def chain_step(a, g, way, step):
        at = slot(way, step)
        block = chain_block(way, step)

        def send(term):
            outbox[a, g, at] = term.astype(jnp.bfloat16)
            chain_copy(a, g, way, step).start()

        def both():
            chain_wait(a, g, way, step - 1)
            send(part[a, block] + inbox[a, g, at - 1].astype(jnp.float32))

        on = chain_on(way, step)
        if step == 0:

            @pl.when(on)
            def _():
                send(part[a, block])

        else:

            @pl.when(on & (z < CHIPS - 1))
            def _():
                both()

            @pl.when(on & (z == CHIPS - 1))
            def _():
                send(part[a, block])

    def chain(a, g, stage):
        chain_step(a, g, DOWN, stage)

    def far_copy(a, g, d, target):
        return remote(
            outbox.at[a, g, d], inbox.at[a, g, d], rs_send.at[a, g, d], rs_recv.at[a, g, d],
            on_chip(target),
        )

    def chain_end(a, g):
        for step in range(chain_hops(DOWN)):

            @pl.when(chain_on(DOWN, step))
            def _():
                chain_copy(a, g, DOWN, step).wait_send()

        for d in FAR:

            @pl.when(z >= d)
            def _():
                far_copy(a, g, d, z - d).wait_send()

    def term_copy(a, g, target, half):
        rows = pl.ds(half * ROWS, ROWS)
        return remote(
            outbox.at[a, g, target, rows], last_in.at[z, core],
            last_send.at[target, half], last_recv.at[z, core], {"seq": target * CORES + half},
        )

    def term_wait(source, half):
        box = last_in.at[source, half]
        remote(
            box, box, last_send.at[source, half], last_recv.at[source, half],
            {"seq": source * CORES + half},
        ).wait_recv()

    def direct(a, g):
        return (a, g) == (0, GROUPS - 1)

    def term_out(a, g, d, term):
        if d == 0:
            own[a, g] = term
            if direct(a, g):
                outbox[a, g, z] = term.astype(jnp.bfloat16)
        elif direct(a, g):
            outbox[a, g, back(d)] = term.astype(jnp.bfloat16)
        elif d in FAR:
            outbox[a, g, d] = term.astype(jnp.bfloat16)
        else:
            part[a, back(d)] = term

    def term_send(a, g, blocks):
        for d in blocks:
            if d in FAR and not direct(a, g):

                @pl.when(z >= d)
                def _():
                    far_copy(a, g, d, z - d).start()

            if d > 0 and direct(a, g):

                @pl.when(z >= d)
                def _():
                    for half in range(CORES):
                        term_copy(a, g, z - d, half).start()

            if d == 0 and direct(a, g):
                term_copy(a, g, z, other).start()

    def term_end(a, g):
        if not direct(a, g):
            chain_end(a, g)
            return

        def one(i, carry):
            for half in range(CORES):
                term_copy(a, g, i, half).wait_send()
            return carry

        lax.fori_loop(0, z, one, 0)
        term_copy(a, g, z, other).wait_send()

    finals, lasts = [], []

    def leave(kind, g, staged, out, wide):
        here = out.at[:, columns((core * GROUPS + g) * wide, wide)]
        local = pltpu.make_async_copy(staged.at[core], here, out_local.at[kind, g])
        far = remote(
            staged.at[other], here, out_send.at[kind, g], out_recv.at[kind, g], sibling
        )
        local.start()
        far.start()
        there = out.at[:, columns((other * GROUPS + g) * wide, wide)]
        finals.append((local, far, kind, g, there))

    def last_sum(a, g):
        last_sums[core] = own[a, g, pl.ds(pl.multiple_of(core * ROWS, ROWS), ROWS), :]
        term_wait(z, other)
        last_sums[other] = last_in[z, other].astype(jnp.float32)

        def one(i, carry):
            source = CHIPS - 1 - i
            for half in range(CORES):
                term_wait(source, half)
                last_sums[half] = last_sums[half] + last_in[source, half].astype(jnp.float32)
            return carry

        lax.fori_loop(0, CHIPS - 1 - z, one, 0)
        for half in range(CORES):
            g_st[a, g, half] = (last_sums[half] * FACTOR).astype(jnp.bfloat16)
            last = pltpu.make_async_copy(
                g_st.at[a, g, half],
                dk_hbm.at[:, columns((half * GROUPS + g) * HD, HD)],
                last_out.at[half],
            )
            last.start()
            lasts.append(last)

    def term_sum(a, g):
        def add(at):
            own[a, g] = own[a, g] + inbox[a, g, at].astype(jnp.float32)

        if direct(a, g):
            last_sum(a, g)
            return

        @pl.when(z < CHIPS - 1)
        def _():
            chain_wait(a, g, DOWN, chain_hops(DOWN) - 1)
            add(slot(DOWN, chain_hops(DOWN) - 1))

        for d in FAR:

            @pl.when(z + d < CHIPS)
            def _():
                far_copy(a, g, d, z).wait_recv()
                add(d)

        total = own[a, g]
        if a == 0:
            total = total * FACTOR
        g_st[a, g] = total.astype(jnp.bfloat16).reshape(CORES, ROWS, HD)
        leave(2 + a, g, g_st.at[a, g], (dk_hbm, dv_hbm)[a], HD)

    def term_last(a, g, _):
        term_sum(a, g)

    def make_bias():
        query = lax.broadcasted_iota(jnp.int32, (1, CHIP_ROWS), 1) + z * CHIP_ROWS
        opening = jnp.zeros((1, CHIP_ROWS), jnp.int32)
        end = jnp.int32(0)
        for d in range(DOCS):
            end = end + doc_ref[pack, d]
            ends = jnp.full((1, CHIP_ROWS), 0, jnp.int32) + end
            opening = jnp.maximum(opening, jnp.where(ends <= query, ends, 0))
        rows = lax.broadcasted_iota(jnp.int32, (CHIP_ROWS, CHIP_ROWS), 0)

        def one(b, carry):
            at = rows + b * CHIP_ROWS
            bias[b] = jnp.where((at >= opening) & (at <= query), 0.0, HIDDEN)
            return carry

        lax.fori_loop(0, CHIPS, one, 0)

    def clear(i, carry):
        for g in range(GROUPS):
            kv[g, i] = jnp.zeros(kv.shape[2:], kv.dtype)
        return carry

    def heads(ref, g):
        parts = [
            ref[g, :, :, h * HD : (h + 1) * HD].reshape(CHIP_ROWS, HD) for h in range(GHEADS)
        ]
        return jnp.concatenate(parts, axis=0)

    def rows_of(a, g, b):
        return kv[g, b, a].reshape(CHIP_ROWS, HD)

    def score_pass(g, blocks):
        @pl.when(z >= blocks[0])
        def _():
            for d in blocks:
                b = back(d)
                hide = jnp.concatenate([bias[b]] * GHEADS, axis=1)
                scores = mm(rows_of(0, g, b), heads(q_s, g), NT) + hide
                peak = fold_rows(scores, jnp.max) * EXP_SCALE
                raised = jnp.exp2(scores * EXP_SCALE - peak)
                p_s[b] = raised
                scale_s[b] = peak
                sum_s[b] = fold_rows(raised, jnp.sum)

        if blocks[0] > 0:

            @pl.when(z < blocks[0])
            def _():
                for d in blocks:
                    b = back(d)
                    scale_s[b] = jnp.full(scale_s.shape[1:], HIDDEN, jnp.float32)
                    sum_s[b] = jnp.zeros(sum_s.shape[1:], jnp.float32)

    def merge_scales():
        peaks = [scale_s[b] for b in range(CHIPS)]
        top = peaks[0]
        for peak in peaks[1:]:
            top = jnp.maximum(top, peak)
        lifts = [jnp.exp2(peak - top) for peak in peaks]
        total = sum_s[0] * lifts[0]
        for b in range(1, CHIPS):
            total = total + sum_s[b] * lifts[b]
        inverse = 1.0 / total
        for b in range(CHIPS):
            scale_s[b] = lifts[b] * inverse

    def value_pass(g, blocks):
        @pl.when(z >= blocks[0])
        def _():
            total = ot_s[...]
            for d in blocks:
                b = back(d)
                weight = p_s[b] * scale_s[b]
                half = weight.astype(jnp.bfloat16)
                total = total + mm(rows_of(1, g, b).T, half, NN)
                term_out(1, g, d, mm(half, heads(do_s, g), NN))
            ot_s[...] = total

        term_send(1, g, blocks)

    def value_end(g):
        for h in range(GHEADS):
            span = slice(h * CHIP_ROWS, (h + 1) * CHIP_ROWS)
            cols = slice(h * HD, (h + 1) * HD)
            out = ot_s[:, span]
            grad = do_s[g, :, :, cols].reshape(CHIP_ROWS, HD).astype(jnp.float32)
            delta_s[:, span] = jnp.sum(out * grad.T, axis=0, keepdims=True)
            o_st[g, :, :, cols] = out.T.astype(jnp.bfloat16).reshape(CORES, ROWS, HD)
        leave(0, g, o_st.at[g], o_hbm, GWIDTH)

    def score_back(g, blocks):
        @pl.when(z >= blocks[0])
        def _():
            late = g == GROUPS - 1
            total = None if late else dqt_s[...]
            for d in blocks:
                b = back(d)
                dweight = mm(rows_of(1, g, b), heads(do_s, g), NT)
                weight = p_s[b] * scale_s[b]
                dscore = (weight * (dweight - delta_s[...])).astype(jnp.bfloat16)
                if late:
                    dscore_s[b] = dscore
                else:
                    total = total + mm(rows_of(0, g, b).T, dscore, NN)
                term_out(0, g, d, mm(dscore, heads(q_s, g), NN))
            if not late:
                dqt_s[...] = total

        term_send(0, g, blocks)

    def query_late(g, blocks):
        @pl.when(z >= blocks[0])
        def _():
            total = dqt_s[...]
            for d in blocks:
                b = back(d)
                total = total + mm(rows_of(0, g, b).T, dscore_s[b], NN)
            dqt_s[...] = total

    def query_end(g):
        for h in range(GHEADS):
            span = slice(h * CHIP_ROWS, (h + 1) * CHIP_ROWS)
            cols = slice(h * HD, (h + 1) * HD)
            grad = (dqt_s[:, span] * FACTOR).T.astype(jnp.bfloat16)
            dq_st[g, :, :, cols] = grad.reshape(CORES, ROWS, HD)
        leave(1, g, dq_st.at[g], dq_hbm, GWIDTH)

    pl.semaphore_wait(barrier, CHIPS * CORES - 1)
    ring(0, 0)
    for key in order:
        swaps[key].start()
    make_bias()
    lax.fori_loop(jnp.maximum(z + 1, HOPS[DOWN]), CHIPS, clear, 0)
    ring(0, 1)
    for n in range(4):
        arrive(n, 0)
    for a in (0, 1):
        arrive(a, 1)
    for step, blocks in enumerate(COMING):
        score_pass(0, blocks)
        if step < 3:
            ring(0, step + 2)
        if step == 1:
            ring(1, 0)
    merge_scales()
    def after(what, g, n):
        if (what, g, n) in AHEAD:
            ring(1, AHEAD[what, g, n])
        for event in EVENTS.get((what, g, n), ()):
            (chain if event[2] < 4 else term_last)(*event)

    for g in range(GROUPS):
        ot_s[...] = jnp.zeros_like(ot_s)
        dqt_s[...] = jnp.zeros_like(dqt_s)
        for n, blocks in enumerate(GOING):
            value_pass(g, blocks)
            after("value", g, n)
        value_end(g)
        for n, blocks in enumerate(GOING):
            score_back(g, blocks)
            after("score", g, n)
        if g == GROUPS - 1:
            for blocks in ((0, 1, 2, 3), (4, 5, 6, 7)):
                query_late(g, blocks)
        query_end(g)
        if g == 0:
            arrive(2, 1)
            arrive(3, 1)
            ring(1, 4)
            for blocks in COMING:
                score_pass(1, blocks)
            merge_scales()
            chain(0, 0, 2)
    term_sum(1, 1)
    term_sum(0, 1)

    for copy in swaps.values():
        copy.wait_send()
    for g in range(GROUPS):
        ring_end(g)
        for a in (0, 1):
            term_end(a, g)
    for copy in lasts:
        copy.wait()
    for local_copy, far, kind, g, there in finals:
        local_copy.wait()
        far.wait_send()
        remote(
            there, there, out_send.at[kind, g], out_recv.at[kind, g], sibling
        ).wait_recv()


def copy_out(*refs):
    count = (len(refs) - 2) // 3
    ins, outs, held = refs[:count], refs[count : 2 * count], refs[2 * count : 3 * count]
    in_sem, out_sem = refs[-2:]
    reads = [pltpu.make_async_copy(ins[i], held[i], in_sem.at[i]) for i in range(count)]
    writes = [pltpu.make_async_copy(held[i], outs[i], out_sem.at[i]) for i in range(count)]
    for read in reads:
        read.start()
    for read, write in zip(reads, writes):
        read.wait()
        write.start()
    for write in writes:
        write.wait()


def local(query_rows, key_rows, value_rows, out_grad, doc_lengths):
    rows = query_rows.shape[1]
    half = jnp.bfloat16
    flat = [x.reshape(rows, x.shape[2]) for x in (query_rows, key_rows, value_rows, out_grad)]
    anywhere = pl.BlockSpec(memory_space=pl.ANY)
    dma = pltpu.SemaphoreType.DMA
    outs = pl.pallas_call(
        kernel,
        out_shape=[
            jax.ShapeDtypeStruct(flat[0].shape, half),
            jax.ShapeDtypeStruct(flat[0].shape, half),
            jax.ShapeDtypeStruct(flat[1].shape, half),
            jax.ShapeDtypeStruct(flat[1].shape, half),
        ],
        in_specs=[anywhere] * 4 + [pl.BlockSpec(memory_space=pltpu.SMEM)],
        out_specs=[anywhere] * 4,
        scratch_shapes=[
            pltpu.VMEM((GROUPS, CORES, ROWS, GWIDTH), half),
            pltpu.VMEM((GROUPS, CORES, ROWS, GWIDTH), half),
            pltpu.VMEM((GROUPS, CHIPS, 2, CORES, ROWS, HD), half),
            pltpu.VMEM((CHIPS, CHIP_ROWS, CHIP_ROWS), jnp.float32),
            pltpu.VMEM((CHIPS, CHIP_ROWS, WIDE), jnp.float32),
            pltpu.VMEM((CHIPS, 1, WIDE), jnp.float32),
            pltpu.VMEM((CHIPS, 1, WIDE), jnp.float32),
            pltpu.VMEM((HD, WIDE), jnp.float32),
            pltpu.VMEM((HD, WIDE), jnp.float32),
            pltpu.VMEM((1, WIDE), jnp.float32),
            pltpu.VMEM((GROUPS, CORES, ROWS, GWIDTH), half),
            pltpu.VMEM((GROUPS, CORES, ROWS, GWIDTH), half),
            pltpu.VMEM((2, CHIPS, CHIP_ROWS, HD), jnp.float32),
            pltpu.VMEM((2, GROUPS, CHIP_ROWS, HD), jnp.float32),
            pltpu.VMEM((2, GROUPS, CHIPS, CHIP_ROWS, HD), half),
            pltpu.VMEM((2, GROUPS, CHIPS, CHIP_ROWS, HD), half),
            pltpu.VMEM((2, GROUPS, CORES, ROWS, HD), half),
            dma((4, GROUPS)), dma((4, GROUPS)), dma((4, GROUPS)),
            dma((GROUPS, 2, 4)), dma((GROUPS, 2, 4)),
            dma((2, GROUPS, CHIPS)), dma((2, GROUPS, CHIPS)),
            dma((4, GROUPS)), dma((4, GROUPS)), dma((4, GROUPS)),
            pltpu.VMEM((CHIPS, CORES, ROWS, HD), half),
            pltpu.VMEM((CORES, ROWS, HD), jnp.float32),
            dma((CHIPS, CORES)), dma((CHIPS, CORES)), dma((CORES,)),
            pltpu.VMEM((CHIPS, CHIP_ROWS, WIDE), half),
            dma((2, 2, CORES)), dma((2, 2, CORES)),
        ],
        compiler_params=pltpu.CompilerParams(
            collective_id=0, has_side_effects=True, vmem_limit_bytes=60 * 2**20
        ),
        name="packed_attention",
    )(*flat, doc_lengths)
    outs = pl.pallas_call(
        copy_out,
        out_shape=[jax.ShapeDtypeStruct(x.shape, x.dtype) for x in outs],
        in_specs=[anywhere] * 4,
        out_specs=[anywhere] * 4,
        scratch_shapes=[pltpu.VMEM(x.shape, x.dtype) for x in outs] + [dma((4,)), dma((4,))],
        name="copy_out",
    )(*outs)
    return tuple(x.reshape(1, rows, x.shape[1]) for x in outs)


def solution(mesh):
    placed = P("dp", "seq", None)
    return jax.shard_map(
        local,
        mesh=mesh,
        in_specs=(placed,) * 4 + (P(),),
        out_specs=(placed,) * 4,
        check_vma=False,
    )
```
